256 devices in a mesh: dp: 16 (over x, y), tensor: 16 (over z, core).
Axes of the slice: x: 4, y: 4, z: 8, core: 2. Of those that a mesh axis runs over, the one named last changes fastest.
Arguments:
- activations: bfloat16 [32, 1024, 28672], P('dp', None, 'tensor'), may hold values from -6 to 6
- out_grads: bfloat16 [32, 1024, 8192], P('dp', None, 'tensor'), may hold values from -6 to 6
- in_factor: bfloat16 [64, 28672], P(None, 'tensor'), may hold values from -0.03125 to 0.03125
- out_factor: bfloat16 [64, 8192], P(None, 'tensor'), may hold values from -0.001953125 to 0.001953125
- queries: bfloat16 [1024, 4096], P('dp', 'tensor'), may hold values from -0.125 to 0.125
Outputs:
- projected_grads: bfloat16 [32, 4096], P('dp', 'tensor')
- scores: float32 [32, 1024], P('dp', 'tensor')
The draws below stay inside these ranges and needn't reach their ends.
All inputs are finite; a program needn't handle non-finite values.
Results may differ from the reference program's by a relative error of at most 0.0057.
Values may be sent and summed in bfloat16 or wider, within the bound.
No kernel may reach another device: no remote copies, remote signals or barrier semaphores. Data moves between devices by JAX's collectives and lax.ppermute only.
A program may use at most 64 MiB of HBM per device.

```python
import jax
import jax.numpy as jnp
from jax import lax

D = 8192
FF = 28672
RANK = 64
GRAD = 4096
SEQ = 1024
EXAMPLES = 32
QUERIES = 1024


def raised(entries, own_key, source, target, shards_of, factor):
    def block_of(position):
        return (jnp.arange(entries.shape[position]) // (entries.shape[position] // shards_of)).reshape((-1,) + (1,) * (entries.ndim - 1 - position))

    first = jax.random.permutation(own_key, shards_of)[block_of(target)]
    second = (block_of(target) + shards_of // 2) % shards_of
    return jnp.where((block_of(source) == first) | (block_of(source) == second), factor * entries, entries)


def shard_levels(stream_key, extent, cuts, least, largest):
    def one(dim, blocks):
        steps = jax.random.uniform(jax.random.fold_in(jax.random.fold_in(stream_key, 6), dim), (blocks,), jnp.float32, least / len(cuts), largest / len(cuts))
        return jnp.repeat(jnp.exp(steps), extent[dim] // blocks).reshape((-1,) + (1,) * (len(extent) - dim - 1))

    loudness = one(*cuts[0])
    for cut in cuts[1:]:
        loudness = loudness * one(*cut)
    return loudness


def noise(key, extent, width, reach, cuts=(), held_as=jnp.bfloat16):
    array = width * jax.random.normal(key, extent, jnp.float32)
    if cuts:
        array = array * shard_levels(key, extent, cuts, -0.22, 0.18)
    return jnp.clip(array, -reach, reach).astype(held_as)


def gaussian_with(own_key, dims, spread, most, shards, heavy, dtype=jnp.bfloat16):
    array = spread * jax.random.normal(own_key, dims, jnp.float32)
    if shards:
        array = array * shard_levels(own_key, dims, shards, -0.22, 0.18)
    return jnp.clip(raised(array, jax.random.fold_in(own_key, 3), *heavy), -most, most).astype(dtype)


def setup_inputs(seed: int = 0) -> dict:
    key_of = jax.random.split(jax.random.key(seed), 6)
    return {
        "activations": noise(key_of[0], (EXAMPLES, SEQ, FF), 1.0, 6.0, ((0, 16), (2, 16))),
        "out_grads": noise(key_of[1], (EXAMPLES, SEQ, D), 1.0, 6.0, ((0, 16), (2, 16))),
        "in_factor": noise(key_of[2], (RANK, FF), FF ** -0.5, 0.03125, ((1, 16),)),
        "out_factor": noise(key_of[3], (RANK, D), (D * SEQ) ** -0.5, 0.001953125, ((1, 16),)),
        "queries": gaussian_with(key_of[4], (QUERIES, GRAD), GRAD ** -0.5, 0.125, ((0, 16), (1, 16)), (1, 0, 16, 2.0)),
    }


def reference(activations, out_grads, in_factor, out_factor, queries):
    def per_example(example_pair):
        example_acts, example_grads = example_pair
        input_proj = jnp.dot(example_acts, in_factor.T, preferred_element_type=jnp.float32).astype(jnp.bfloat16)
        grad_proj = jnp.dot(example_grads, out_factor.T, preferred_element_type=jnp.float32).astype(jnp.bfloat16)
        product = jnp.dot(input_proj.T, grad_proj, preferred_element_type=jnp.float32)
        return product.reshape(-1).astype(jnp.bfloat16)

    projected_grads = lax.map(per_example, (activations, out_grads))
    scores = jnp.dot(projected_grads, queries.T, preferred_element_type=jnp.float32)
    return projected_grads, scores
```

```python
import jax
import jax.numpy as jnp
import numpy as np
from jax import lax
from jax.experimental import pallas as pl
from jax.experimental.pallas import tpu as pltpu
from jax.sharding import PartitionSpec as P

RANK = 64
LANES = 128
F32 = jnp.float32
BF16 = jnp.bfloat16
MIB = 1024 * 1024
NT = (((1,), (1,)), ((), ()))
TN = (((0,), (0,)), ((), ()))
SMEM = pl.BlockSpec(memory_space=pltpu.SMEM)
VMEM = pl.BlockSpec(memory_space=pltpu.VMEM)
ANY = pl.BlockSpec(memory_space=pl.ANY)


def shaped(shape, dtype):
    return jax.ShapeDtypeStruct(shape, dtype)


def project_kernel(which, acts, grads, inf, outf, out):
    del which
    left = lax.dot_general(acts[0], inf[...], NT, preferred_element_type=F32)
    right = lax.dot_general(grads[0], outf[...], NT, preferred_element_type=F32)
    out[...] = jnp.concatenate([left, right], axis=1)


def project(which, acts, grads, inf, outf):
    _, seq, ff = acts.shape
    d = grads.shape[2]
    rows = seq // 2
    held = [pltpu.with_memory_space_constraint(x, pltpu.HBM) for x in (acts, grads, inf, outf)]
    return pl.pallas_call(
        project_kernel,
        out_shape=pltpu.VMEM((seq, 2 * RANK), F32),
        grid_spec=pltpu.PrefetchScalarGridSpec(
            num_scalar_prefetch=1,
            grid=(seq // rows,),
            in_specs=[
                pl.BlockSpec((1, rows, ff), lambda i, w: (w[0], i, 0)),
                pl.BlockSpec((1, rows, d), lambda i, w: (w[0], i, 0)),
                pl.BlockSpec((RANK, ff), lambda i, w: (0, 0)),
                pl.BlockSpec((RANK, d), lambda i, w: (0, 0)),
            ],
            out_specs=pl.BlockSpec((rows, 2 * RANK), lambda i, w: (i, 0)),
        ),
        compiler_params=pltpu.CompilerParams(vmem_limit_bytes=24 * MIB),
        cost_estimate=pl.CostEstimate(
            flops=2 * seq * (ff + d) * RANK,
            bytes_accessed=2 * seq * (ff + d),
            transcendentals=0,
        ),
        name="project",
    )(which, *held)


def pair_kernel(kept, arrived, block, out, same):
    out[...] = (kept[...] + arrived[...]).astype(BF16)
    same[...] = block[...]


def pair_sum(kept, arrived, block):
    return pl.pallas_call(
        pair_kernel,
        out_shape=(shaped(kept.shape, BF16), shaped(block.shape, BF16)),
        in_specs=[VMEM] * 3,
        out_specs=(VMEM, VMEM),
        compiler_params=pltpu.CompilerParams(vmem_limit_bytes=8 * MIB),
        name="pair_sum",
    )(kept, arrived, block)


def product_kernel(parts, *refs):
    blocks = refs[:-3]
    out, joined, square = refs[-3:]
    total = jnp.sum(parts[...].astype(F32), axis=0)
    square[...] = lax.dot_general(
        total[:, :RANK],
        total[:, RANK:],
        TN,
        precision=lax.Precision.HIGHEST,
        preferred_element_type=F32,
    )
    half = RANK // 2
    rows = jnp.concatenate(
        [square[pl.ds(0, half, stride=2), :], square[pl.ds(1, half, stride=2), :]], axis=1
    )
    for copy in range(out.shape[0]):
        out[copy] = rows
    for n, block in enumerate(blocks):
        joined[n] = block[...]


def product(parts, copies, blocks):
    return pl.pallas_call(
        product_kernel,
        out_shape=(
            shaped((copies, RANK * RANK // LANES, LANES), F32),
            shaped((len(blocks),) + blocks[0].shape, BF16),
        ),
        in_specs=[VMEM] * (1 + len(blocks)),
        out_specs=(VMEM, VMEM),
        scratch_shapes=[pltpu.VMEM((RANK, RANK), F32)],
        compiler_params=pltpu.CompilerParams(vmem_limit_bytes=8 * MIB),
        name="product",
    )(parts, *blocks)


def finish_kernel(place, parts, *refs):
    pieces = refs[:-3]
    gradients, scores, held = refs[-3:]
    tensor = place[0]
    devices, rows, _ = parts.shape
    for example in range(2):
        total = parts[example]
        for z in range(1, devices // 2):
            total = total + parts[2 * z + example]
        held[example * rows : (example + 1) * rows] = total.astype(BF16).astype(F32)
    blocks = rows // devices
    mine = [
        jnp.concatenate(
            [held[pl.ds(e * rows + tensor * blocks + b, 1), :] for b in range(blocks)], axis=1
        )
        for e in range(2)
    ]
    gradients[...] = jnp.concatenate(mine, axis=0).astype(BF16)
    sums = [jnp.zeros((scores.shape[1], LANES), F32) for _ in range(2)]
    at = 0
    for piece in pieces:
        for n in range(piece.shape[0]):
            at += 1
            owner = place[at]
            for b in range(blocks):
                q = piece[n, :, b * LANES : (b + 1) * LANES].astype(F32)
                for e in range(2):
                    sums[e] = sums[e] + q * held[pl.ds(e * rows + owner * blocks + b, 1), :]
    for e in range(2):
        scores[e : e + 1, :] = jnp.sum(sums[e].T, axis=0, keepdims=True)


def finish(place, parts, pieces):
    _, rows, _ = parts.shape
    _, count, width = pieces[0].shape
    return pl.pallas_call(
        finish_kernel,
        out_shape=(shaped((2, width), BF16), shaped((2, count), F32)),
        in_specs=[SMEM, VMEM] + [VMEM] * len(pieces),
        out_specs=(VMEM, VMEM),
        scratch_shapes=[pltpu.VMEM((2 * rows, LANES), F32)],
        compiler_params=pltpu.CompilerParams(vmem_limit_bytes=8 * MIB),
        name="finish",
    )(place, parts, *pieces)


def stops(n_dp, n_tensor):
    chips, side = n_tensor // 2, 4

    def ring(a, n):
        return min(a % n, -a % n)

    shifts = sorted(range(n_dp), key=lambda s: (ring(s // side, side) + ring(s % side, side), s))
    table = np.zeros((n_tensor, n_dp), np.int32)
    for m in range(n_tensor):
        far = sorted(range(n_tensor), key=lambda k: (-ring(k // 2 - m // 2, chips), k))
        for k, shift in zip(far, shifts):
            x, y = (m // side + shift // side) % side, (m % side + shift % side) % side
            table[m, x * side + y] = k
    return table


def local(activations, out_grads, in_factor, out_factor, queries):
    n_dp, n_tensor = lax.axis_size("dp"), lax.axis_size("tensor")
    dp, tensor = lax.axis_index("dp"), lax.axis_index("tensor")
    core = tensor % 2
    chips = n_tensor // 2

    def swapped(x, bits):
        return lax.ppermute(x, "dp", [(i, i ^ bits) for i in range(n_dp)])

    arrays = (activations, out_grads, in_factor, out_factor)
    sent = project((1 - core).reshape(1), *arrays)
    arrived = lax.ppermute(sent, "tensor", [(i, i ^ 1) for i in range(n_tensor)])
    table = stops(n_dp, n_tensor)
    moves = [
        (m * n_tensor + int(table[m, j]), j * n_tensor + m)
        for m in range(n_tensor)
        for j in range(n_dp)
    ]
    turned = lax.ppermute(queries, ("dp", "tensor"), moves)
    kept = project(core.reshape(1), *arrays)
    pair, block = pair_sum(kept, arrived, turned)

    along_z = [[2 * z + c for z in range(chips)] for c in range(2)]
    tokens = pair.shape[0] // chips
    shares = lax.all_to_all(
        pair.reshape(chips, tokens, 2 * RANK), "tensor", 0, 0, axis_index_groups=along_z
    )
    blocks = [block] + [swapped(block, bits) for bits in (1, 2, 3)]
    copies, four = product(shares, n_tensor, blocks)
    everyone = lax.all_to_all(copies, "tensor", 0, 0)
    rest = [swapped(four, 4 * b) for b in range(1, n_dp // 4)]
    order = jnp.asarray(table)[tensor, lax.bitwise_xor(dp, jnp.arange(n_dp))]
    place = jnp.concatenate([tensor.reshape(1), order]).astype(jnp.int32)
    return finish(place, everyone, [four] + rest)


def solution(mesh):
    placed = (
        P("dp", None, "tensor"),
        P("dp", None, "tensor"),
        P(None, "tensor"),
        P(None, "tensor"),
        P("dp", "tensor"),
    )
    return jax.shard_map(
        local,
        mesh=mesh,
        in_specs=placed,
        out_specs=(P("dp", "tensor"), P("dp", "tensor")),
        check_vma=False,
    )
```

```python
import jax
import jax.numpy as jnp
from jax import lax
from jax.experimental import pallas as pl
from jax.experimental.pallas import tpu as pltpu
from jax.sharding import PartitionSpec as P

RANK = 64
LANES = 128
F32 = jnp.float32
BF16 = jnp.bfloat16
MIB = 1024 * 1024
FORWARD = 20000000000
HOLD = 1000000000
SENT = jnp.bfloat16
NT = (((1,), (1,)), ((), ()))
TN = (((0,), (0,)), ((), ()))
SMEM = pl.BlockSpec(memory_space=pltpu.SMEM)
VMEM = pl.BlockSpec(memory_space=pltpu.VMEM)
ANY = pl.BlockSpec(memory_space=pl.ANY)


def shaped(shape, dtype):
    return jax.ShapeDtypeStruct(shape, dtype)


def project_kernel(which, acts, grads, inf, outf, block, out, same):
    del which
    same[...] = block[...]
    left = lax.dot_general(acts[0], inf[...], NT, preferred_element_type=F32)
    right = lax.dot_general(grads[0], outf[...], NT, preferred_element_type=F32)
    out[...] = jnp.concatenate([left, right], axis=1)


def project(which, acts, grads, inf, outf, block):
    _, seq, ff = acts.shape
    d = grads.shape[2]
    rows = seq // 2
    held = [
        pltpu.with_memory_space_constraint(x, pltpu.HBM) for x in (acts, grads, inf, outf, block)
    ]
    return pl.pallas_call(
        project_kernel,
        out_shape=(
            pltpu.VMEM((seq, 2 * RANK), F32),
            pltpu.VMEM(block.shape, block.dtype),
        ),
        grid_spec=pltpu.PrefetchScalarGridSpec(
            num_scalar_prefetch=1,
            grid=(seq // rows,),
            in_specs=[
                pl.BlockSpec((1, rows, ff), lambda i, w: (w[0], i, 0)),
                pl.BlockSpec((1, rows, d), lambda i, w: (w[0], i, 0)),
                pl.BlockSpec((RANK, ff), lambda i, w: (0, 0)),
                pl.BlockSpec((RANK, d), lambda i, w: (0, 0)),
                pl.BlockSpec(block.shape, lambda i, w: (0, 0)),
            ],
            out_specs=(
                pl.BlockSpec((rows, 2 * RANK), lambda i, w: (i, 0)),
                pl.BlockSpec(block.shape, lambda i, w: (0, 0)),
            ),
        ),
        compiler_params=pltpu.CompilerParams(vmem_limit_bytes=24 * MIB),
        cost_estimate=pl.CostEstimate(
            flops=20 * seq * (ff + d) * RANK,
            bytes_accessed=2 * seq * (ff + d),
            transcendentals=0,
        ),
        name="project",
    )(which, *held)


def whole_kernel(which, acts, grads, inf, outf, out):
    left = lax.dot_general(acts[which[0]], inf[...], NT, preferred_element_type=F32)
    right = lax.dot_general(grads[which[0]], outf[...], NT, preferred_element_type=F32)
    out[...] = jnp.concatenate([left, right], axis=1)


def project_whole(which, acts, grads, inf, outf):
    _, seq, ff = acts.shape
    d = grads.shape[2]
    held = [pltpu.with_memory_space_constraint(x, pltpu.VMEM) for x in (acts, grads, inf, outf)]
    return pl.pallas_call(
        whole_kernel,
        out_shape=pltpu.VMEM((seq, 2 * RANK), F32),
        in_specs=[SMEM, VMEM, VMEM, VMEM, VMEM],
        out_specs=VMEM,
        compiler_params=pltpu.CompilerParams(vmem_limit_bytes=24 * MIB),
        cost_estimate=pl.CostEstimate(
            flops=1 * 2 * seq * (ff + d) * RANK,
            bytes_accessed=2 * seq * (ff + d),
            transcendentals=0,
        ),
        name="project_whole",
    )(which, *held)


def pair_kernel(kept, arrived, out):
    out[...] = (kept[...] + arrived[...]).astype(BF16)


def pair_sum(kept, arrived):
    return pl.pallas_call(
        pair_kernel,
        out_shape=shaped(kept.shape, BF16),
        in_specs=[VMEM] * 2,
        out_specs=VMEM,
        compiler_params=pltpu.CompilerParams(vmem_limit_bytes=8 * MIB),
        name="pair_sum",
    )(kept, arrived)


def forward_kernel(block, after, out):
    del after
    out[...] = block[...]


def forward(block, after):
    return pl.pallas_call(
        forward_kernel,
        out_shape=shaped(block.shape, block.dtype),
        in_specs=[VMEM, ANY],
        out_specs=VMEM,
        compiler_params=pltpu.CompilerParams(vmem_limit_bytes=8 * MIB),
        cost_estimate=pl.CostEstimate(flops=FORWARD, bytes_accessed=0, transcendentals=0),
        name="forward",
    )(block, after)


def join_kernel(*refs):
    out = refs[-1]
    for n, block in enumerate(refs[:-1]):
        out[n] = block[...]


def join(blocks):
    return pl.pallas_call(
        join_kernel,
        out_shape=shaped((len(blocks),) + blocks[0].shape, BF16),
        in_specs=[VMEM] * len(blocks),
        out_specs=VMEM,
        compiler_params=pltpu.CompilerParams(vmem_limit_bytes=8 * MIB),
        name="join",
    )(*blocks)


def hold_kernel(place, after, out):
    del after
    for n in range(place.shape[0]):
        out[n] = place[n]


def hold(place, after):
    return pl.pallas_call(
        hold_kernel,
        out_shape=shaped(place.shape, place.dtype),
        in_specs=[SMEM, ANY],
        out_specs=SMEM,
        cost_estimate=pl.CostEstimate(flops=HOLD, bytes_accessed=0, transcendentals=0),
        compiler_params=pltpu.CompilerParams(vmem_limit_bytes=8 * MIB),
        name="hold",
    )(place, after)


def product_kernel(parts, queries, out, same, square):
    total = jnp.sum(parts[...].astype(F32), axis=0)
    square[...] = lax.dot_general(
        total[:, :RANK],
        total[:, RANK:],
        TN,
        precision=lax.Precision.HIGHEST,
        preferred_element_type=F32,
    )
    half = RANK // 2
    rows = jnp.concatenate(
        [square[pl.ds(0, half, stride=2), :], square[pl.ds(1, half, stride=2), :]], axis=1
    ).astype(out.dtype)
    for copy in range(out.shape[0]):
        out[copy] = rows
    same[...] = queries[...]


def product(parts, copies, queries):
    return pl.pallas_call(
        product_kernel,
        out_shape=(
            shaped((copies, RANK * RANK // LANES, LANES), SENT),
            shaped(queries.shape, queries.dtype),
        ),
        in_specs=[VMEM, VMEM],
        out_specs=(VMEM, VMEM),
        scratch_shapes=[pltpu.VMEM((RANK, RANK), F32)],
        compiler_params=pltpu.CompilerParams(vmem_limit_bytes=8 * MIB),
        name="product",
    )(parts, queries)


def finish_kernel(place, parts, *refs):
    pieces = refs[:-3]
    gradients, scores, held = refs[-3:]
    dp, tensor = place[0], place[1]
    near = near_stops(parts.shape[0])
    halves = [sum(r << (4 * n) for n, r in enumerate(near[at : at + 8])) for at in (0, 8)]
    halves = [jnp.int32(h - (1 << 32) if h >> 31 else h) for h in halves]

    def lookup(shift):
        half = jnp.where(shift < 8, halves[0], halves[1])
        return lax.shift_right_logical(half, 4 * (shift & 7)) & 15

    devices, rows, _ = parts.shape
    for example in range(2):
        total = parts[example].astype(F32)
        for z in range(1, devices // 2):
            total = total + parts[2 * z + example].astype(F32)
        held[example * rows : (example + 1) * rows] = total.astype(BF16).astype(F32)
    blocks = rows // devices
    mine = [
        jnp.concatenate(
            [held[pl.ds(e * rows + tensor * blocks + b, 1), :] for b in range(blocks)], axis=1
        )
        for e in range(2)
    ]
    gradients[...] = jnp.concatenate(mine, axis=0).astype(BF16)
    sums = [jnp.zeros((scores.shape[1], LANES), F32) for _ in range(2)]
    at = 0
    for piece in pieces:
        for n in range(piece.shape[0]):
            owner = source(tensor, lax.bitwise_xor(dp, jnp.int32(at)), lookup)
            at += 1
            for b in range(blocks):
                q = piece[n, :, b * LANES : (b + 1) * LANES].astype(F32)
                for e in range(2):
                    sums[e] = sums[e] + q * held[pl.ds(e * rows + owner * blocks + b, 1), :]
    for e in range(2):
        scores[e : e + 1, :] = jnp.sum(sums[e].T, axis=0, keepdims=True)


def finish(place, parts, pieces):
    _, rows, _ = parts.shape
    _, count, width = pieces[0].shape
    return pl.pallas_call(
        finish_kernel,
        out_shape=(shaped((2, width), BF16), shaped((2, count), F32)),
        in_specs=[SMEM, VMEM] + [VMEM] * len(pieces),
        out_specs=(VMEM, VMEM),
        scratch_shapes=[pltpu.VMEM((2 * rows, LANES), F32)],
        compiler_params=pltpu.CompilerParams(vmem_limit_bytes=8 * MIB),
        name="finish",
    )(place, parts, *pieces)


def ring(a, n):
    return min(a % n, -a % n)


def near_stops(n_tensor):
    shifts = sorted(range(16), key=lambda s: (ring(s // 4, 4) + ring(s % 4, 4), s))
    far = sorted(range(n_tensor), key=lambda r: (-ring(r // 2, n_tensor // 2), r))
    return [r for _, r in sorted(zip(shifts, far))]


def source(m, j, lookup):
    shift = (((j >> 2) - (m >> 2)) & 3) * 4 + ((j - m) & 3)
    r = lookup(shift)
    return (((m >> 1) + (r >> 1)) & 7) * 2 + (r & 1)


def local(activations, out_grads, in_factor, out_factor, queries):
    n_dp, n_tensor = lax.axis_size("dp"), lax.axis_size("tensor")
    dp, tensor = lax.axis_index("dp"), lax.axis_index("tensor")
    core = tensor % 2
    chips = n_tensor // 2

    def swapped(x, bits):
        return lax.ppermute(x, "dp", [(i, i ^ bits) for i in range(n_dp)])

    arrays = (activations, out_grads, in_factor, out_factor)
    sent, block = project((1 - core).reshape(1), *arrays, queries)
    arrived = lax.ppermute(sent, "tensor", [(i, i ^ 1) for i in range(n_tensor)])
    near = near_stops(n_tensor)
    moves = [
        (m * n_tensor + source(m, j, near.__getitem__), j * n_tensor + m)
        for m in range(n_tensor)
        for j in range(n_dp)
    ]
    turned = lax.ppermute(block, ("dp", "tensor"), moves)
    kept = project_whole(core.reshape(1), *arrays)
    pair = pair_sum(kept, arrived)
    block = forward(turned, pair)

    along_z = [[2 * z + c for z in range(chips)] for c in range(2)]
    tokens = pair.shape[0] // chips
    shares = lax.all_to_all(
        pair.reshape(chips, tokens, 2 * RANK), "tensor", 0, 0, axis_index_groups=along_z
    )
    four = join([block] + [swapped(block, bits) for bits in (1, 2, 3)])
    two = swapped(four, 8)
    copies, same = product(shares, n_tensor, four)
    everyone = lax.all_to_all(copies, "tensor", 0, 0)
    one, three = swapped(same, 4), swapped(same, 12)
    place = hold(jnp.stack([dp, tensor]).astype(jnp.int32), two)
    return finish(place, everyone, [same, one, two, three])


def solution(mesh):
    placed = (
        P("dp", None, "tensor"),
        P("dp", None, "tensor"),
        P(None, "tensor"),
        P(None, "tensor"),
        P("dp", "tensor"),
    )
    return jax.shard_map(
        local,
        mesh=mesh,
        in_specs=placed,
        out_specs=(P("dp", "tensor"), P("dp", "tensor")),
        check_vma=False,
    )
```

```python
import jax
import jax.numpy as jnp
from jax import lax
from jax.experimental import pallas as pl
from jax.experimental.pallas import tpu as pltpu
from jax.sharding import PartitionSpec as P

RANK = 64
LANES = 128
F32 = jnp.float32
BF16 = jnp.bfloat16
MIB = 1024 * 1024
FORWARD = 20_000_000_000
SENT = jnp.bfloat16
NEAR = (0, 13, 12, 1)
FAR = (0, 7, 4, 3)
NT = (((1,), (1,)), ((), ()))
TN = (((0,), (0,)), ((), ()))
VMEM = pl.BlockSpec(memory_space=pltpu.VMEM)
ANY = pl.BlockSpec(memory_space=pl.ANY)


def shaped(shape, dtype):
    return jax.ShapeDtypeStruct(shape, dtype)


def own_core():
    return lax.axis_index("tensor") % 2


def project_kernel(acts, grads, inf, outf, block, out, same):
    same[...] = block[...]
    left = lax.dot_general(acts[0], inf[...], NT, preferred_element_type=F32)
    right = lax.dot_general(grads[0], outf[...], NT, preferred_element_type=F32)
    out[...] = jnp.concatenate([left, right], axis=1)


def project(acts, grads, inf, outf, block):
    _, seq, ff = acts.shape
    d = grads.shape[2]
    rows = seq // 2
    held = [
        pltpu.with_memory_space_constraint(x, pltpu.HBM) for x in (acts, grads, inf, outf, block)
    ]
    return pl.pallas_call(
        project_kernel,
        out_shape=(
            pltpu.VMEM((seq, 2 * RANK), F32),
            pltpu.VMEM(block.shape, block.dtype),
        ),
        grid=(seq // rows,),
        in_specs=[
            pl.BlockSpec((1, rows, ff), lambda i: (1 - own_core(), i, 0)),
            pl.BlockSpec((1, rows, d), lambda i: (1 - own_core(), i, 0)),
            pl.BlockSpec((RANK, ff), lambda i: (0, 0)),
            pl.BlockSpec((RANK, d), lambda i: (0, 0)),
            pl.BlockSpec(block.shape, lambda i: (0, 0)),
        ],
        out_specs=(
            pl.BlockSpec((rows, 2 * RANK), lambda i: (i, 0)),
            pl.BlockSpec(block.shape, lambda i: (0, 0)),
        ),
        compiler_params=pltpu.CompilerParams(vmem_limit_bytes=24 * MIB),
        cost_estimate=pl.CostEstimate(
            flops=20 * seq * (ff + d) * RANK,
            bytes_accessed=2 * seq * (ff + d),
            transcendentals=0,
        ),
        name="project",
    )(*held)


def whole_kernel(acts, grads, inf, outf, out):
    left = lax.dot_general(acts[own_core()], inf[...], NT, preferred_element_type=F32)
    right = lax.dot_general(grads[own_core()], outf[...], NT, preferred_element_type=F32)
    out[...] = jnp.concatenate([left, right], axis=1)


def project_whole(acts, grads, inf, outf):
    _, seq, ff = acts.shape
    d = grads.shape[2]
    held = [pltpu.with_memory_space_constraint(x, pltpu.VMEM) for x in (acts, grads, inf, outf)]
    return pl.pallas_call(
        whole_kernel,
        out_shape=pltpu.VMEM((seq, 2 * RANK), F32),
        in_specs=[VMEM, VMEM, VMEM, VMEM],
        out_specs=VMEM,
        compiler_params=pltpu.CompilerParams(vmem_limit_bytes=24 * MIB),
        cost_estimate=pl.CostEstimate(
            flops=1 * 2 * seq * (ff + d) * RANK,
            bytes_accessed=2 * seq * (ff + d),
            transcendentals=0,
        ),
        name="project_whole",
    )(*held)


def pair_kernel(kept, arrived, out):
    out[...] = (kept[...] + arrived[...]).astype(BF16)


def pair_sum(kept, arrived):
    return pl.pallas_call(
        pair_kernel,
        out_shape=shaped(kept.shape, BF16),
        in_specs=[VMEM] * 2,
        out_specs=VMEM,
        compiler_params=pltpu.CompilerParams(vmem_limit_bytes=8 * MIB),
        name="pair_sum",
    )(kept, arrived)


def forward_kernel(block, after, out):
    del after
    out[...] = block[...]


def forward(block, after):
    return pl.pallas_call(
        forward_kernel,
        out_shape=shaped(block.shape, block.dtype),
        in_specs=[VMEM, ANY],
        out_specs=VMEM,
        compiler_params=pltpu.CompilerParams(vmem_limit_bytes=8 * MIB),
        cost_estimate=pl.CostEstimate(flops=FORWARD, bytes_accessed=0, transcendentals=0),
        name="forward",
    )(block, after)


def join_kernel(*refs):
    out = refs[-1]
    for n, block in enumerate(refs[:-1]):
        out[n] = block[...]


def join(blocks):
    return pl.pallas_call(
        join_kernel,
        out_shape=shaped((len(blocks),) + blocks[0].shape, BF16),
        in_specs=[VMEM] * len(blocks),
        out_specs=VMEM,
        compiler_params=pltpu.CompilerParams(vmem_limit_bytes=8 * MIB),
        name="join",
    )(*blocks)


def product_kernel(parts, queries, out, same, square):
    total = jnp.sum(parts[...].astype(F32), axis=0)
    square[...] = lax.dot_general(
        total[:, :RANK],
        total[:, RANK:],
        TN,
        precision=lax.Precision.HIGHEST,
        preferred_element_type=F32,
    )
    half = RANK // 2
    rows = jnp.concatenate(
        [square[pl.ds(0, half, stride=2), :], square[pl.ds(1, half, stride=2), :]], axis=1
    ).astype(out.dtype)
    for copy in range(out.shape[0]):
        out[copy] = rows
    same[...] = queries[...]


def product(parts, copies, queries):
    return pl.pallas_call(
        product_kernel,
        out_shape=(
            shaped((copies, RANK * RANK // LANES, LANES), SENT),
            shaped(queries.shape, queries.dtype),
        ),
        in_specs=[VMEM, VMEM],
        out_specs=(VMEM, VMEM),
        scratch_shapes=[pltpu.VMEM((RANK, RANK), F32)],
        compiler_params=pltpu.CompilerParams(vmem_limit_bytes=8 * MIB),
        name="product",
    )(parts, queries)


def finish_kernel(parts, *refs):
    pieces = refs[:-3]
    gradients, scores, held = refs[-3:]
    dp, tensor = lax.axis_index("dp"), lax.axis_index("tensor")
    near = near_stops(parts.shape[0])
    halves = [sum(r << (4 * n) for n, r in enumerate(near[at : at + 8])) for at in (0, 8)]
    halves = [jnp.int32(h - (1 << 32) if h >> 31 else h) for h in halves]

    def lookup(shift):
        half = jnp.where(shift < 8, halves[0], halves[1])
        return lax.shift_right_logical(half, 4 * (shift & 7)) & 15

    devices, rows, _ = parts.shape
    for example in range(2):
        total = parts[example].astype(F32)
        for z in range(1, devices // 2):
            total = total + parts[2 * z + example].astype(F32)
        held[example * rows : (example + 1) * rows] = total.astype(BF16).astype(F32)
    blocks = rows // devices
    mine = [
        jnp.concatenate(
            [held[pl.ds(e * rows + tensor * blocks + b, 1), :] for b in range(blocks)], axis=1
        )
        for e in range(2)
    ]
    gradients[...] = jnp.concatenate(mine, axis=0).astype(BF16)
    sums = [jnp.zeros((scores.shape[1], LANES), F32) for _ in range(2)]
    for far, piece in zip(FAR, pieces):
        for n, near_bits in enumerate(NEAR):
            owner = source(tensor, lax.bitwise_xor(dp, jnp.int32(far ^ near_bits)), lookup)
            for b in range(blocks):
                q = piece[n, :, b * LANES : (b + 1) * LANES].astype(F32)
                for e in range(2):
                    sums[e] = sums[e] + q * held[pl.ds(e * rows + owner * blocks + b, 1), :]
    for e in range(2):
        scores[e : e + 1, :] = jnp.sum(sums[e].T, axis=0, keepdims=True)


def finish(parts, pieces):
    _, rows, _ = parts.shape
    _, count, width = pieces[0].shape
    return pl.pallas_call(
        finish_kernel,
        out_shape=(shaped((2, width), BF16), shaped((2, count), F32)),
        in_specs=[VMEM] * (1 + len(pieces)),
        out_specs=(VMEM, VMEM),
        scratch_shapes=[pltpu.VMEM((2 * rows, LANES), F32)],
        compiler_params=pltpu.CompilerParams(vmem_limit_bytes=8 * MIB),
        name="finish",
    )(parts, *pieces)


def ring(a, n):
    return min(a % n, -a % n)


def near_stops(n_tensor):
    shifts = sorted(range(16), key=lambda s: (ring(s // 4, 4) + ring(s % 4, 4), s))
    far = sorted(range(n_tensor), key=lambda r: (-ring(r // 2, n_tensor // 2), r))
    return [r for _, r in sorted(zip(shifts, far))]


def source(m, j, lookup):
    shift = (((j >> 2) - (m >> 2)) & 3) * 4 + ((j - m) & 3)
    r = lookup(shift)
    return (((m >> 1) + (r >> 1)) & 7) * 2 + (r & 1)


def local(activations, out_grads, in_factor, out_factor, queries):
    n_dp, n_tensor = lax.axis_size("dp"), lax.axis_size("tensor")
    chips = n_tensor // 2

    def swapped(x, bits):
        return lax.ppermute(x, "dp", [(i, i ^ bits) for i in range(n_dp)])

    arrays = (activations, out_grads, in_factor, out_factor)
    sent, block = project(*arrays, queries)
    arrived = lax.ppermute(sent, "tensor", [(i, i ^ 1) for i in range(n_tensor)])
    near = near_stops(n_tensor)
    moves = [
        (m * n_tensor + source(m, j, near.__getitem__), j * n_tensor + m)
        for m in range(n_tensor)
        for j in range(n_dp)
    ]
    turned = lax.ppermute(block, ("dp", "tensor"), moves)
    kept = project_whole(*arrays)
    pair = pair_sum(kept, arrived)
    block = forward(turned, pair)

    along_z = [[2 * z + c for z in range(chips)] for c in range(2)]
    tokens = pair.shape[0] // chips
    shares = lax.all_to_all(
        pair.reshape(chips, tokens, 2 * RANK), "tensor", 0, 0, axis_index_groups=along_z
    )
    four = join([block] + [swapped(block, bits) for bits in NEAR[1:]])
    copies, same = product(shares, n_tensor, four)
    everyone = lax.all_to_all(copies, "tensor", 0, 0)
    return finish(everyone, [same] + [swapped(same, bits) for bits in FAR[1:]])


def solution(mesh):
    placed = (
        P("dp", None, "tensor"),
        P("dp", None, "tensor"),
        P(None, "tensor"),
        P(None, "tensor"),
        P("dp", "tensor"),
    )
    return jax.shard_map(
        local,
        mesh=mesh,
        in_specs=placed,
        out_specs=(P("dp", "tensor"), P("dp", "tensor")),
        check_vma=False,
    )
```

```python
import jax
import jax.numpy as jnp
from jax import lax
from jax.experimental import pallas as pl
from jax.experimental.pallas import tpu as pltpu
from jax.sharding import PartitionSpec as P

RANK = 64
LANES = 128
F32 = jnp.float32
BF16 = jnp.bfloat16
MIB = 1024 * 1024
FORWARD = 20_000_000_000
SENT = jnp.bfloat16
NEAR = (0, 13, 12, 1)
FAR = (0, 7, 4, 3)
NT = (((1,), (1,)), ((), ()))
TN = (((0,), (0,)), ((), ()))
VMEM = pl.BlockSpec(memory_space=pltpu.VMEM)
ANY = pl.BlockSpec(memory_space=pl.ANY)


def shaped(shape, dtype):
    return jax.ShapeDtypeStruct(shape, dtype)


def own_core():
    return lax.axis_index("tensor") % 2


def project_kernel(acts, grads, inf, outf, out):
    left = lax.dot_general(acts[0], inf[...], NT, preferred_element_type=F32)
    right = lax.dot_general(grads[0], outf[...], NT, preferred_element_type=F32)
    out[...] = jnp.concatenate([left, right], axis=1)


def project(acts, grads, inf, outf):
    _, seq, ff = acts.shape
    d = grads.shape[2]
    rows = seq // 2
    held = [pltpu.with_memory_space_constraint(x, pltpu.HBM) for x in (acts, grads, inf, outf)]
    return pl.pallas_call(
        project_kernel,
        out_shape=pltpu.VMEM((seq, 2 * RANK), F32),
        grid=(seq // rows,),
        in_specs=[
            pl.BlockSpec((1, rows, ff), lambda i: (1 - own_core(), i, 0)),
            pl.BlockSpec((1, rows, d), lambda i: (1 - own_core(), i, 0)),
            pl.BlockSpec((RANK, ff), lambda i: (0, 0)),
            pl.BlockSpec((RANK, d), lambda i: (0, 0)),
        ],
        out_specs=pl.BlockSpec((rows, 2 * RANK), lambda i: (i, 0)),
        compiler_params=pltpu.CompilerParams(vmem_limit_bytes=24 * MIB),
        cost_estimate=pl.CostEstimate(
            flops=20 * seq * (ff + d) * RANK,
            bytes_accessed=2 * seq * (ff + d),
            transcendentals=0,
        ),
        name="project",
    )(*held)


def whole_kernel(acts, grads, inf, outf, out):
    left = lax.dot_general(acts[own_core()], inf[...], NT, preferred_element_type=F32)
    right = lax.dot_general(grads[own_core()], outf[...], NT, preferred_element_type=F32)
    out[...] = jnp.concatenate([left, right], axis=1)


def project_whole(acts, grads, inf, outf):
    _, seq, ff = acts.shape
    d = grads.shape[2]
    held = [pltpu.with_memory_space_constraint(x, pltpu.VMEM) for x in (acts, grads, inf, outf)]
    return pl.pallas_call(
        whole_kernel,
        out_shape=pltpu.VMEM((seq, 2 * RANK), F32),
        in_specs=[VMEM, VMEM, VMEM, VMEM],
        out_specs=VMEM,
        compiler_params=pltpu.CompilerParams(vmem_limit_bytes=24 * MIB),
        cost_estimate=pl.CostEstimate(
            flops=1 * 2 * seq * (ff + d) * RANK,
            bytes_accessed=2 * seq * (ff + d),
            transcendentals=0,
        ),
        name="project_whole",
    )(*held)


def pair_kernel(kept, arrived, out):
    out[...] = (kept[...] + arrived[...]).astype(BF16)


def pair_sum(kept, arrived):
    return pl.pallas_call(
        pair_kernel,
        out_shape=shaped(kept.shape, BF16),
        in_specs=[VMEM] * 2,
        out_specs=VMEM,
        compiler_params=pltpu.CompilerParams(vmem_limit_bytes=8 * MIB),
        name="pair_sum",
    )(kept, arrived)


def forward_kernel(block, after, out):
    del after
    out[...] = block[...]


def forward(block, after):
    return pl.pallas_call(
        forward_kernel,
        out_shape=shaped(block.shape, block.dtype),
        in_specs=[VMEM, ANY],
        out_specs=VMEM,
        compiler_params=pltpu.CompilerParams(vmem_limit_bytes=8 * MIB),
        cost_estimate=pl.CostEstimate(flops=FORWARD, bytes_accessed=0, transcendentals=0),
        name="forward",
    )(block, after)


def join_kernel(*refs):
    out = refs[-1]
    for n, block in enumerate(refs[:-1]):
        out[n] = block[...]


def join(blocks):
    return pl.pallas_call(
        join_kernel,
        out_shape=shaped((len(blocks),) + blocks[0].shape, BF16),
        in_specs=[VMEM] * len(blocks),
        out_specs=VMEM,
        compiler_params=pltpu.CompilerParams(vmem_limit_bytes=8 * MIB),
        name="join",
    )(*blocks)


def product_kernel(parts, queries, out, same, square):
    total = jnp.sum(parts[...].astype(F32), axis=0)
    high = total.astype(BF16)
    low = (total - high.astype(F32)).astype(BF16)
    left = jnp.concatenate([high[:, :RANK], high[:, :RANK], low[:, :RANK]], axis=0)
    right = jnp.concatenate([high[:, RANK:], low[:, RANK:], high[:, RANK:]], axis=0)
    square[...] = lax.dot_general(left, right, TN, preferred_element_type=F32)
    half = RANK // 2
    rows = jnp.concatenate(
        [square[pl.ds(0, half, stride=2), :], square[pl.ds(1, half, stride=2), :]], axis=1
    ).astype(out.dtype)
    for copy in range(out.shape[0]):
        out[copy] = rows
    same[...] = queries[...]


def product(parts, copies, queries):
    return pl.pallas_call(
        product_kernel,
        out_shape=(
            shaped((copies, RANK * RANK // LANES, LANES), SENT),
            shaped(queries.shape, queries.dtype),
        ),
        in_specs=[VMEM, VMEM],
        out_specs=(VMEM, VMEM),
        scratch_shapes=[pltpu.VMEM((RANK, RANK), F32)],
        compiler_params=pltpu.CompilerParams(vmem_limit_bytes=8 * MIB),
        name="product",
    )(parts, queries)


def finish_kernel(parts, *refs):
    pieces = refs[:-3]
    gradients, scores, held = refs[-3:]
    dp, tensor = lax.axis_index("dp"), lax.axis_index("tensor")
    near = near_stops(parts.shape[0])
    halves = [sum(r << (4 * n) for n, r in enumerate(near[at : at + 8])) for at in (0, 8)]
    halves = [jnp.int32(h - (1 << 32) if h >> 31 else h) for h in halves]

    def lookup(shift):
        half = jnp.where(shift < 8, halves[0], halves[1])
        return lax.shift_right_logical(half, 4 * (shift & 7)) & 15

    devices, rows, _ = parts.shape
    for example in range(2):
        total = parts[example].astype(F32)
        for z in range(1, devices // 2):
            total = total + parts[2 * z + example].astype(F32)
        held[example * rows : (example + 1) * rows] = total.astype(BF16).astype(F32)
    blocks = rows // devices
    mine = [
        jnp.concatenate(
            [held[pl.ds(e * rows + tensor * blocks + b, 1), :] for b in range(blocks)], axis=1
        )
        for e in range(2)
    ]
    gradients[...] = jnp.concatenate(mine, axis=0).astype(BF16)
    sums = [jnp.zeros((scores.shape[1], LANES), F32) for _ in range(2)]
    for far, piece in zip(FAR, pieces):
        for n, near_bits in enumerate(NEAR):
            owner = source(tensor, lax.bitwise_xor(dp, jnp.int32(far ^ near_bits)), lookup)
            for b in range(blocks):
                q = piece[n, :, b * LANES : (b + 1) * LANES].astype(F32)
                for e in range(2):
                    sums[e] = sums[e] + q * held[pl.ds(e * rows + owner * blocks + b, 1), :]
    for e in range(2):
        scores[e : e + 1, :] = jnp.sum(sums[e].T, axis=0, keepdims=True)


def finish(parts, pieces):
    _, rows, _ = parts.shape
    _, count, width = pieces[0].shape
    return pl.pallas_call(
        finish_kernel,
        out_shape=(shaped((2, width), BF16), shaped((2, count), F32)),
        in_specs=[VMEM] * (1 + len(pieces)),
        out_specs=(VMEM, VMEM),
        scratch_shapes=[pltpu.VMEM((2 * rows, LANES), F32)],
        compiler_params=pltpu.CompilerParams(vmem_limit_bytes=8 * MIB),
        name="finish",
    )(parts, *pieces)


def ring(a, n):
    return min(a % n, -a % n)


def near_stops(n_tensor):
    shifts = sorted(range(16), key=lambda s: (ring(s // 4, 4) + ring(s % 4, 4), s))
    far = sorted(range(n_tensor), key=lambda r: (-ring(r // 2, n_tensor // 2), r))
    return [r for _, r in sorted(zip(shifts, far))]


def source(m, j, lookup):
    shift = (((j >> 2) - (m >> 2)) & 3) * 4 + ((j - m) & 3)
    r = lookup(shift)
    return (((m >> 1) + (r >> 1)) & 7) * 2 + (r & 1)


def local(activations, out_grads, in_factor, out_factor, queries):
    n_dp, n_tensor = lax.axis_size("dp"), lax.axis_size("tensor")
    chips = n_tensor // 2

    def swapped(x, bits):
        return lax.ppermute(x, "dp", [(i, i ^ bits) for i in range(n_dp)])

    arrays = (activations, out_grads, in_factor, out_factor)
    sent = project(*arrays)
    arrived = lax.ppermute(sent, "tensor", [(i, i ^ 1) for i in range(n_tensor)])
    near = near_stops(n_tensor)
    moves = [
        (m * n_tensor + source(m, j, near.__getitem__), j * n_tensor + m)
        for m in range(n_tensor)
        for j in range(n_dp)
    ]
    turned = lax.ppermute(queries, ("dp", "tensor"), moves)
    kept = project_whole(*arrays)
    pair = pair_sum(kept, arrived)
    block = forward(turned, pair)

    along_z = [[2 * z + c for z in range(chips)] for c in range(2)]
    tokens = pair.shape[0] // chips
    shares = lax.all_to_all(
        pair.reshape(chips, tokens, 2 * RANK), "tensor", 0, 0, axis_index_groups=along_z
    )
    four = join([block] + [swapped(block, bits) for bits in NEAR[1:]])
    copies, same = product(shares, n_tensor, four)
    everyone = lax.all_to_all(copies, "tensor", 0, 0)
    return finish(everyone, [same] + [swapped(same, bits) for bits in FAR[1:]])


def solution(mesh):
    placed = (
        P("dp", None, "tensor"),
        P("dp", None, "tensor"),
        P(None, "tensor"),
        P(None, "tensor"),
        P("dp", "tensor"),
    )
    return jax.shard_map(
        local,
        mesh=mesh,
        in_specs=placed,
        out_specs=(P("dp", "tensor"), P("dp", "tensor")),
        check_vma=False,
    )
```

```python
import jax
import jax.numpy as jnp
from jax import lax
from jax.experimental import pallas as pl
from jax.experimental.pallas import tpu as pltpu
from jax.sharding import PartitionSpec as P

RANK = 64
LANES = 128
F32 = jnp.float32
BF16 = jnp.bfloat16
MIB = 1024 * 1024
FORWARD = 20_000_000_000
SENT = jnp.bfloat16
NEAR = (0, 13, 12, 1)
FAR = (0, 7, 4, 3)
NT = (((1,), (1,)), ((), ()))
TN = (((0,), (0,)), ((), ()))
VMEM = pl.BlockSpec(memory_space=pltpu.VMEM)
ANY = pl.BlockSpec(memory_space=pl.ANY)


def shaped(shape, dtype):
    return jax.ShapeDtypeStruct(shape, dtype)


def own_core():
    return lax.axis_index("tensor") % 2


def project_kernel(acts, grads, inf, outf, block, out, same):
    same[...] = block[...]
    left = lax.dot_general(acts[0], inf[...], NT, preferred_element_type=F32)
    right = lax.dot_general(grads[0], outf[...], NT, preferred_element_type=F32)
    out[...] = jnp.concatenate([left, right], axis=1)


def project(acts, grads, inf, outf, block):
    _, seq, ff = acts.shape
    d = grads.shape[2]
    rows = seq // 2
    held = [
        pltpu.with_memory_space_constraint(x, pltpu.HBM) for x in (acts, grads, inf, outf, block)
    ]
    return pl.pallas_call(
        project_kernel,
        out_shape=(
            pltpu.VMEM((seq, 2 * RANK), F32),
            pltpu.VMEM(block.shape, block.dtype),
        ),
        grid=(seq // rows,),
        in_specs=[
            pl.BlockSpec((1, rows, ff), lambda i: (1 - own_core(), i, 0)),
            pl.BlockSpec((1, rows, d), lambda i: (1 - own_core(), i, 0)),
            pl.BlockSpec((RANK, ff), lambda i: (0, 0)),
            pl.BlockSpec((RANK, d), lambda i: (0, 0)),
            pl.BlockSpec(block.shape, lambda i: (0, 0)),
        ],
        out_specs=(
            pl.BlockSpec((rows, 2 * RANK), lambda i: (i, 0)),
            pl.BlockSpec(block.shape, lambda i: (0, 0)),
        ),
        compiler_params=pltpu.CompilerParams(vmem_limit_bytes=24 * MIB),
        cost_estimate=pl.CostEstimate(
            flops=20 * seq * (ff + d) * RANK,
            bytes_accessed=2 * seq * (ff + d),
            transcendentals=0,
        ),
        name="project",
    )(*held)


def whole_kernel(acts, grads, inf, outf, out):
    left = lax.dot_general(acts[own_core()], inf[...], NT, preferred_element_type=F32)
    right = lax.dot_general(grads[own_core()], outf[...], NT, preferred_element_type=F32)
    out[...] = jnp.concatenate([left, right], axis=1)


def project_whole(acts, grads, inf, outf):
    _, seq, ff = acts.shape
    d = grads.shape[2]
    held = [pltpu.with_memory_space_constraint(x, pltpu.VMEM) for x in (acts, grads, inf, outf)]
    return pl.pallas_call(
        whole_kernel,
        out_shape=pltpu.VMEM((seq, 2 * RANK), F32),
        in_specs=[VMEM, VMEM, VMEM, VMEM],
        out_specs=VMEM,
        compiler_params=pltpu.CompilerParams(vmem_limit_bytes=24 * MIB),
        cost_estimate=pl.CostEstimate(
            flops=1 * 2 * seq * (ff + d) * RANK,
            bytes_accessed=2 * seq * (ff + d),
            transcendentals=0,
        ),
        name="project_whole",
    )(*held)


def pair_kernel(kept, arrived, out):
    out[...] = (kept[...] + arrived[...]).astype(BF16)


def pair_sum(kept, arrived):
    return pl.pallas_call(
        pair_kernel,
        out_shape=shaped(kept.shape, BF16),
        in_specs=[VMEM] * 2,
        out_specs=VMEM,
        compiler_params=pltpu.CompilerParams(vmem_limit_bytes=8 * MIB),
        name="pair_sum",
    )(kept, arrived)


def forward_kernel(block, after, out):
    del after
    out[...] = block[...]


def forward(block, after):
    return pl.pallas_call(
        forward_kernel,
        out_shape=shaped(block.shape, block.dtype),
        in_specs=[VMEM, ANY],
        out_specs=VMEM,
        compiler_params=pltpu.CompilerParams(vmem_limit_bytes=8 * MIB),
        cost_estimate=pl.CostEstimate(flops=FORWARD, bytes_accessed=0, transcendentals=0),
        name="forward",
    )(block, after)


def join_kernel(*refs):
    out = refs[-1]
    for n, block in enumerate(refs[:-1]):
        out[n] = block[...]


def join(blocks):
    return pl.pallas_call(
        join_kernel,
        out_shape=shaped((len(blocks),) + blocks[0].shape, BF16),
        in_specs=[VMEM] * len(blocks),
        out_specs=VMEM,
        compiler_params=pltpu.CompilerParams(vmem_limit_bytes=8 * MIB),
        name="join",
    )(*blocks)


def product_kernel(parts, queries, out, same, square):
    total = jnp.sum(parts[...].astype(F32), axis=0)
    high = total.astype(BF16)
    low = (total - high.astype(F32)).astype(BF16)
    left = jnp.concatenate([high[:, :RANK], high[:, :RANK], low[:, :RANK]], axis=0)
    right = jnp.concatenate([high[:, RANK:], low[:, RANK:], high[:, RANK:]], axis=0)
    square[...] = lax.dot_general(left, right, TN, preferred_element_type=F32)
    half = RANK // 2
    rows = jnp.concatenate(
        [square[pl.ds(0, half, stride=2), :], square[pl.ds(1, half, stride=2), :]], axis=1
    ).astype(out.dtype)
    for copy in range(out.shape[0]):
        out[copy] = rows
    same[...] = queries[...]


def product(parts, copies, queries):
    return pl.pallas_call(
        product_kernel,
        out_shape=(
            shaped((copies, RANK * RANK // LANES, LANES), SENT),
            shaped(queries.shape, queries.dtype),
        ),
        in_specs=[VMEM, VMEM],
        out_specs=(VMEM, VMEM),
        scratch_shapes=[pltpu.VMEM((RANK, RANK), F32)],
        compiler_params=pltpu.CompilerParams(vmem_limit_bytes=8 * MIB),
        name="product",
    )(parts, queries)


def finish_kernel(parts, *refs):
    pieces = refs[:-3]
    gradients, scores, held = refs[-3:]
    dp, tensor = lax.axis_index("dp"), lax.axis_index("tensor")
    near = near_stops(parts.shape[0])
    halves = [sum(r << (4 * n) for n, r in enumerate(near[at : at + 8])) for at in (0, 8)]
    halves = [jnp.int32(h - (1 << 32) if h >> 31 else h) for h in halves]

    def lookup(shift):
        half = jnp.where(shift < 8, halves[0], halves[1])
        return lax.shift_right_logical(half, 4 * (shift & 7)) & 15

    devices, rows, _ = parts.shape
    for example in range(2):
        total = parts[example].astype(F32)
        for z in range(1, devices // 2):
            total = total + parts[2 * z + example].astype(F32)
        held[example * rows : (example + 1) * rows] = total.astype(BF16).astype(F32)
    blocks = rows // devices
    mine = [
        jnp.concatenate(
            [held[pl.ds(e * rows + tensor * blocks + b, 1), :] for b in range(blocks)], axis=1
        )
        for e in range(2)
    ]
    gradients[...] = jnp.concatenate(mine, axis=0).astype(BF16)
    sums = [jnp.zeros((scores.shape[1], LANES), F32) for _ in range(2)]
    for far, piece in zip(FAR, pieces):
        for n, near_bits in enumerate(NEAR):
            owner = source(tensor, lax.bitwise_xor(dp, jnp.int32(far ^ near_bits)), lookup)
            for b in range(blocks):
                q = piece[n, :, b * LANES : (b + 1) * LANES].astype(F32)
                for e in range(2):
                    sums[e] = sums[e] + q * held[pl.ds(e * rows + owner * blocks + b, 1), :]
    for e in range(2):
        scores[e : e + 1, :] = jnp.sum(sums[e].T, axis=0, keepdims=True)


def finish(parts, pieces):
    _, rows, _ = parts.shape
    _, count, width = pieces[0].shape
    return pl.pallas_call(
        finish_kernel,
        out_shape=(shaped((2, width), BF16), shaped((2, count), F32)),
        in_specs=[VMEM] * (1 + len(pieces)),
        out_specs=(VMEM, VMEM),
        scratch_shapes=[pltpu.VMEM((2 * rows, LANES), F32)],
        compiler_params=pltpu.CompilerParams(vmem_limit_bytes=8 * MIB),
        name="finish",
    )(parts, *pieces)


def ring(a, n):
    return min(a % n, -a % n)


def near_stops(n_tensor):
    shifts = sorted(range(16), key=lambda s: (ring(s // 4, 4) + ring(s % 4, 4), s))
    far = sorted(range(n_tensor), key=lambda r: (-ring(r // 2, n_tensor // 2), r))
    return [r for _, r in sorted(zip(shifts, far))]


def source(m, j, lookup):
    shift = (((j >> 2) - (m >> 2)) & 3) * 4 + ((j - m) & 3)
    r = lookup(shift)
    return (((m >> 1) + (r >> 1)) & 7) * 2 + (r & 1)


def local(activations, out_grads, in_factor, out_factor, queries):
    n_dp, n_tensor = lax.axis_size("dp"), lax.axis_size("tensor")
    chips = n_tensor // 2

    def swapped(x, bits):
        return lax.ppermute(x, "dp", [(i, i ^ bits) for i in range(n_dp)])

    arrays = (activations, out_grads, in_factor, out_factor)
    sent, block = project(*arrays, queries)
    arrived = lax.ppermute(sent, "tensor", [(i, i ^ 1) for i in range(n_tensor)])
    near = near_stops(n_tensor)
    moves = [
        (m * n_tensor + source(m, j, near.__getitem__), j * n_tensor + m)
        for m in range(n_tensor)
        for j in range(n_dp)
    ]
    turned = lax.ppermute(block, ("dp", "tensor"), moves)
    kept = project_whole(*arrays)
    pair = pair_sum(kept, arrived)
    block = forward(turned, pair)

    along_z = [[2 * z + c for z in range(chips)] for c in range(2)]
    tokens = pair.shape[0] // chips
    shares = lax.all_to_all(
        pair.reshape(chips, tokens, 2 * RANK), "tensor", 0, 0, axis_index_groups=along_z
    )
    four = join([block] + [swapped(block, bits) for bits in NEAR[1:]])
    copies, same = product(shares, n_tensor, four)
    everyone = lax.all_to_all(copies, "tensor", 0, 0)
    return finish(everyone, [same] + [swapped(same, bits) for bits in FAR[1:]])


def solution(mesh):
    placed = (
        P("dp", None, "tensor"),
        P("dp", None, "tensor"),
        P(None, "tensor"),
        P(None, "tensor"),
        P("dp", "tensor"),
    )
    return jax.shard_map(
        local,
        mesh=mesh,
        in_specs=placed,
        out_specs=(P("dp", "tensor"), P("dp", "tensor")),
        check_vma=False,
    )
```
